32 devices in a mesh: groups: 2 (over x), rows: 16 (over z, y, core).
Axes of the slice: x: 2, y: 2, z: 4, core: 2. Of those that a mesh axis runs over, the one named last changes fastest.
Arguments:
- row_leaves: int32 [32, 65536], P(None, ('groups', 'rows')), parts along dimension 1, may hold values from 0 to 127
- covariates: bfloat16 [64, 65536], P(None, ('groups', 'rows')), parts along dimension 1, may hold values from -6 to 6
- query_leaves: int32 [32, 128], P(None, 'groups'), parts along dimension 1, may hold values from 0 to 127
- leaf_sizes: int32 [64, 128], P('groups'), parts along dimension 0, may hold values from 128 to 511
Outputs:
- moments: float32 [128, 4096], P(('groups', 'rows')), parts along dimension 0
The draws below stay inside these ranges and needn't reach their ends.
There are 2 independent parts, one for each index of `groups`. The reference program is written for one: setup_inputs(seed, part) draws one part's arguments, and reference() takes and returns one part's arrays. A program takes and returns all parts, laid end to end along the dimension named above; each array names one. Nothing has to cross between parts.
All inputs are finite; a program needn't handle non-finite values.
Results may differ from the reference program's by a relative error of at most 0.0006.
Values may be sent and summed in bfloat16 or wider, within the bound.
No kernel may reach another device: no remote copies, remote signals or barrier semaphores. Data moves between devices by JAX's collectives and lax.ppermute only.
A program may use at most 64 MiB of HBM per device.

```python
import math
import jax
import jax.numpy as jnp
import numpy as np
from jax import lax

P_SIZE = 64
LEAVES = 128
TREES = 32
ROWS = 32768
Q = 64


def touch_ends(drawn, stream_key, least, high):
    longest = drawn.shape.index(max(drawn.shape))
    spots = []
    for shift in (0, 1):
        where = [jax.random.randint(jax.random.fold_in(stream_key, axis), (), 0, length) for axis, length in enumerate(drawn.shape)]
        where[longest] = (where[longest] + shift) % drawn.shape[longest]
        spots.append(tuple(where))
    return drawn.at[spots[0]].set(least).at[spots[1]].set(high)


def level_of(rng, dims, shards, low, largest):
    loudness = 1.0
    for dim, blocks in shards:
        heights = jax.random.uniform(jax.random.fold_in(jax.random.fold_in(rng, 6), dim), (blocks,), jnp.float32, low / len(shards), largest / len(shards))
        loudness = loudness * jnp.repeat(jnp.exp(heights), dims[dim] // blocks).reshape((-1,) + (1,) * (len(dims) - 1 - dim))
    return loudness


def cumulative_ranks(amount, slope):
    portions = [(1 << 20) // math.isqrt(grade ** slope) + 1 for grade in range(1, amount + 1)]
    width = 1 + sum(portions) // (1 << 30)
    return np.cumsum(np.array([max(1, weight // width) for weight in portions]))


def skewed_ids(own_key, shape, number_of, lean):
    listing = cumulative_ranks(number_of, lean)
    pick = jax.random.randint(jax.random.fold_in(own_key, 1), shape, 0, int(listing[number_of - 1]))
    standing = jnp.searchsorted(jnp.asarray(listing, jnp.int32), pick, side="right")
    return jax.random.permutation(jax.random.fold_in(own_key, 2), number_of)[standing].astype(jnp.int32)


def normal_values(own_key, shape, scale, reach, shards=(), held_as=jnp.bfloat16):
    entries = scale * jax.random.normal(own_key, shape, jnp.float32)
    if shards:
        entries = entries * level_of(own_key, shape, shards, -0.22, 0.18)
    return jnp.clip(entries, -reach, reach).astype(held_as)


def setup_inputs(seed: int = 0, part: int = 0) -> dict:
    splits = jax.random.split(jax.random.key(seed), 5)
    part_splits = jax.random.split(jax.random.fold_in(splits[4], part), 5)
    return {
        "row_leaves": touch_ends(jax.random.randint(part_splits[0], (TREES, ROWS), 0, LEAVES), jax.random.fold_in(part_splits[0], 1), 0, LEAVES - 1).astype(jnp.int32),
        "covariates": normal_values(part_splits[1], (P_SIZE, ROWS), 1.0, 6.0, ((1, 16),)),
        "query_leaves": touch_ends(skewed_ids(part_splits[2], (TREES, Q), LEAVES, 2), jax.random.fold_in(part_splits[2], 3), 0, LEAVES - 1).astype(jnp.int32),
        "leaf_sizes": touch_ends(jax.random.randint(part_splits[3], (TREES, LEAVES), ROWS // LEAVES // 2, 2 * ROWS // LEAVES), jax.random.fold_in(part_splits[3], 1), ROWS // LEAVES // 2, (2 * ROWS // LEAVES) - 1).astype(jnp.int32),
    }


def reference(row_leaves, covariates, query_leaves, leaf_sizes):
    inverse = 1.0 / (TREES * leaf_sizes.astype(jnp.float32))
    chosen = jnp.take_along_axis(inverse, query_leaves, axis=1).astype(jnp.bfloat16)
    chosen = lax.optimization_barrier(chosen).astype(jnp.float32)
    row_block = math.gcd(ROWS, 2048)
    count_blocks = ROWS // row_block
    leaf_blocks = jnp.transpose(row_leaves.reshape(TREES, count_blocks, row_block), (1, 0, 2))
    covar_blocks = jnp.transpose(covariates.reshape(P_SIZE, count_blocks, row_block), (1, 0, 2))

    def step(summed, inputs):
        leaf_block, covar_block = inputs
        match = query_leaves[:, :, None] == leaf_block[:, None, :]
        weights = jnp.sum(jnp.where(match, chosen[:, :, None], jnp.float32(0.0)), axis=0).astype(jnp.bfloat16)
        widened = covar_block.astype(jnp.float32)
        product = (widened[:, None, :] * widened[None, :, :]).reshape(P_SIZE * P_SIZE, row_block).astype(jnp.bfloat16)
        summed = summed + lax.dot_general(weights, product, (((1,), (1,)), ((), ())), preferred_element_type=jnp.float32)
        return summed, None

    summed, _ = lax.scan(step, jnp.zeros((Q, P_SIZE * P_SIZE), jnp.float32), (leaf_blocks, covar_blocks))
    return summed
```

```python
import functools
import math

import jax
import jax.numpy as jnp
from jax import lax
from jax.experimental import pallas as pl
from jax.experimental.pallas import tpu as pltpu
from jax.sharding import PartitionSpec as P

SUB = 8
LANES = 128
NT = (((1,), (1,)), ((), ()))


def segments(width):
    found, offset = [], 0
    for j in range(width):
        first = j // SUB * SUB
        found.append((offset, first))
        offset += width - first
    return found, offset


def stages(count):
    bits = [1 << i for i in range(count.bit_length() - 1)]
    rest = bits[1:]
    return [bits[:1]] * (count > 1) + [rest[i : i + 2] for i in range(0, len(rest), 2)]


def block_order(count):
    order = [0]
    for group in reversed(stages(count)):
        shifts = [sum(b for i, b in enumerate(group) if (s >> i) & 1) for s in range(1 << len(group))]
        order = [s | p for s in shifts for p in order]
    return order


def moments_kernel(axis, order, unit, rl_ref, x_ref, ql_ref, ls_ref, *out_refs):
    trees, rows = rl_ref.shape
    width = x_ref.shape[0]
    queries = ql_ref.shape[1]
    share = queries // len(order)
    me = lax.axis_index(axis)

    span = max(queries, LANES)
    place = lax.broadcasted_iota(jnp.int32, (trees, span), 1)
    block = jnp.zeros((trees, span), jnp.int32)
    for i in range(len(order).bit_length() - 1):
        block += ((place // share >> i) & 1) * order[1 << i]
    source = ((block ^ me) * share + place % share) % queries
    leaves = ql_ref[...]
    if queries < span:
        leaves = jnp.concatenate([leaves] * (span // queries), axis=1)
    inverse = 1.0 / (trees * ls_ref[...].astype(jnp.float32))
    leaf_parts, weight_parts = [], []
    for part in range(span // LANES):
        at = source[:, part * LANES : (part + 1) * LANES]
        taken = jnp.zeros((trees, LANES), jnp.int32)
        for piece in range(span // LANES):
            got = jnp.take_along_axis(leaves[:, piece * LANES : (piece + 1) * LANES], at % LANES, axis=1)
            taken = jnp.where(at // LANES == piece, got, taken)
        weight = jnp.take_along_axis(inverse, taken, axis=1).astype(jnp.bfloat16).astype(jnp.float32)
        leaf_parts.append(taken.T)
        weight_parts.append((weight.T * unit).astype(jnp.int32))
    leaf = jnp.concatenate(leaf_parts, 0)[:queries].astype(jnp.int16)
    weight = jnp.concatenate(weight_parts, 0)[:queries].astype(jnp.int16)

    step, tall = 256, 32
    for start in range(0, rows, step):
        here = slice(start, start + step)
        row_leaf = rl_ref[:, here].astype(jnp.int16)
        parts = []
        for top in range(0, queries, tall):
            total = jnp.zeros((tall, step), jnp.int16)
            for b in range(trees):
                want = jnp.broadcast_to(leaf[top : top + tall, b : b + 1], (tall, step))
                gives = jnp.broadcast_to(weight[top : top + tall, b : b + 1], (tall, step))
                have = jnp.broadcast_to(row_leaf[b : b + 1], (tall, step))
                total += jnp.where(have == want, gives, jnp.int16(0))
            parts.append((total.astype(jnp.float32) * (1.0 / unit)).astype(jnp.bfloat16))
        kernel_weight = jnp.concatenate(parts, 0)
        wide = x_ref[:, here].astype(jnp.float32)
        row_moments = jnp.concatenate([wide[j : j + 1] * wide[j // SUB * SUB :] for j in range(width)], 0)
        row_moments = row_moments.astype(jnp.bfloat16)
        product = lax.dot_general(kernel_weight, row_moments, NT, preferred_element_type=jnp.float32)
        top = 0
        for ref in out_refs:
            piece = product[top : top + ref.shape[0]]
            ref[...] = piece if start == 0 else ref[...] + piece
            top += ref.shape[0]


def expand_kernel(width, first_ref, second_ref, out_ref, held, full):
    share = out_ref.shape[0]
    total = first_ref[...] + second_ref[...]
    where, _ = segments(width)
    for j in range(width):
        offset, first = where[j]
        held[j, :, first:width] = total[:, offset : offset + width - first]
    upper = lax.broadcasted_iota(jnp.int32, (width, width), 1) >= lax.broadcasted_iota(
        jnp.int32, (width, width), 0
    )
    for q in range(share):
        square = held[:, q, :width]
        full[:, q, :width] = jnp.where(upper, square, square.T)
    for j in range(width):
        out_ref[:, j * width : (j + 1) * width] = full[j, :, :width]


def per_device(row_leaves, covariates, query_leaves, leaf_sizes):
    axis = "rows"
    count = lax.axis_size(axis)
    trees, local_rows = row_leaves.shape
    width = covariates.shape[0]
    queries = query_leaves.shape[1]
    leaves = leaf_sizes.shape[1]
    share = queries // count
    _, columns = segments(width)
    least = local_rows * count // leaves // 2
    unit = float(trees * least * 512)
    order = block_order(count)
    groups = stages(count)

    half = queries // 2
    held, sent = pl.pallas_call(
        functools.partial(moments_kernel, axis, order, unit),
        out_shape=[jax.ShapeDtypeStruct((half, columns), jnp.float32)] * 2,
        compiler_params=pltpu.CompilerParams(vmem_limit_bytes=40 << 20),
        cost_estimate=pl.CostEstimate(
            flops=2 * queries * columns * local_rows,
            bytes_accessed=1 << 20,
            transcendentals=0,
        ),
        name="moments",
    )(row_leaves, covariates, query_leaves, leaf_sizes)

    def permute(array, shift):
        return lax.ppermute(array, axis, [(i, i ^ shift) for i in range(count)])

    first, second = held, permute(sent, groups[0][0])
    for group in groups[1:]:
        total = first + second
        blocks = 1 << len(group)
        size = total.shape[0] // blocks
        arrived = []
        for s in range(1, blocks):
            shift = sum(b for i, b in enumerate(group) if (s >> i) & 1)
            arrived.append(permute(total[s * size : (s + 1) * size], shift))
        first = total[:size]
        for extra in arrived[:-1]:
            first = first + extra
        second = arrived[-1]

    return pl.pallas_call(
        functools.partial(expand_kernel, width),
        out_shape=jax.ShapeDtypeStruct((share, width * width), jnp.float32),
        scratch_shapes=[pltpu.VMEM((width, share, LANES), jnp.float32)] * 2,
        name="expand",
    )(first, second)


def solution(mesh):
    return jax.shard_map(
        per_device,
        mesh=mesh,
        in_specs=(
            P(None, ("groups", "rows")),
            P(None, ("groups", "rows")),
            P(None, "groups"),
            P("groups", None),
        ),
        out_specs=P(("groups", "rows"), None),
        check_vma=False,
    )
```

```python
import functools
import math

import jax
import jax.numpy as jnp
from jax import lax
from jax.experimental import pallas as pl
from jax.experimental.pallas import tpu as pltpu
from jax.sharding import PartitionSpec as P

SUB = 8
LANES = 128
NT = (((1,), (1,)), ((), ()))


def segments(width):
    found, offset = [], 0
    for j in range(width):
        first = j // SUB * SUB
        found.append((offset, first))
        offset += width - first
    return found, offset


def stages(count):
    bits = [1 << i for i in range(count.bit_length() - 1)]
    rest = bits[1:]
    return [bits[:1]] * (count > 1) + [rest[i : i + 2] for i in range(0, len(rest), 2)]


def block_order(count):
    order = [0]
    for group in reversed(stages(count)):
        shifts = [sum(b for i, b in enumerate(group) if (s >> i) & 1) for s in range(1 << len(group))]
        order = [s | p for s in shifts for p in order]
    return order


def moments_kernel(axis, order, unit, step, rl_hbm, x_hbm, ql_hbm, ls_hbm, *refs):
    *out_refs, rl_ref, x_ref, ql_ref, ls_ref, small, large = refs
    trees, rows = rl_ref.shape
    width = x_ref.shape[0]
    queries = ql_ref.shape[1]
    share = queries // len(order)
    me = lax.axis_index(axis)

    copies = [
        pltpu.make_async_copy(ql_hbm, ql_ref, small.at[0]),
        pltpu.make_async_copy(ls_hbm, ls_ref, small.at[1]),
    ]
    pairs = []
    for n, start in enumerate(range(0, rows, step)):
        here = slice(start, start + step)
        pairs.append(
            (
                pltpu.make_async_copy(rl_hbm.at[:, here], rl_ref.at[:, here], large.at[n, 0]),
                pltpu.make_async_copy(x_hbm.at[:, here], x_ref.at[:, here], large.at[n, 1]),
            )
        )
    for copy in copies + [copy for pair in pairs for copy in pair]:
        copy.start()
    for copy in copies:
        copy.wait()

    span = max(queries, LANES)
    place = lax.broadcasted_iota(jnp.int32, (trees, span), 1)
    block = jnp.zeros((trees, span), jnp.int32)
    for i in range(len(order).bit_length() - 1):
        block += ((place // share >> i) & 1) * order[1 << i]
    source = ((block ^ me) * share + place % share) % queries
    leaves = ql_ref[...]
    if queries < span:
        leaves = jnp.concatenate([leaves] * (span // queries), axis=1)
    inverse = 1.0 / (trees * ls_ref[...].astype(jnp.float32))
    leaf_parts, weight_parts = [], []
    for part in range(span // LANES):
        at = source[:, part * LANES : (part + 1) * LANES]
        taken = jnp.zeros((trees, LANES), jnp.int32)
        for piece in range(span // LANES):
            got = jnp.take_along_axis(leaves[:, piece * LANES : (piece + 1) * LANES], at % LANES, axis=1)
            taken = jnp.where(at // LANES == piece, got, taken)
        weight = jnp.take_along_axis(inverse, taken, axis=1).astype(jnp.bfloat16).astype(jnp.float32)
        leaf_parts.append(taken.T)
        weight_parts.append((weight.T * unit).astype(jnp.int32))
    leaf = jnp.concatenate(leaf_parts, 0)[:queries].astype(jnp.int16)
    weight = jnp.concatenate(weight_parts, 0)[:queries].astype(jnp.int16)

    tall = 32
    for n, start in enumerate(range(0, rows, step)):
        here = slice(start, start + step)
        for copy in pairs[n]:
            copy.wait()
        row_leaf = rl_ref[:, here].astype(jnp.int16)
        parts = []
        for top in range(0, queries, tall):
            total = jnp.zeros((tall, step), jnp.int16)
            for b in range(trees):
                want = jnp.broadcast_to(leaf[top : top + tall, b : b + 1], (tall, step))
                gives = jnp.broadcast_to(weight[top : top + tall, b : b + 1], (tall, step))
                have = jnp.broadcast_to(row_leaf[b : b + 1], (tall, step))
                total += jnp.where(have == want, gives, jnp.int16(0))
            parts.append((total.astype(jnp.float32) * (1.0 / unit)).astype(jnp.bfloat16))
        kernel_weight = jnp.concatenate(parts, 0)
        wide = x_ref[:, here].astype(jnp.float32)
        row_moments = jnp.concatenate([wide[j : j + 1] * wide[j // SUB * SUB :] for j in range(width)], 0)
        row_moments = row_moments.astype(jnp.bfloat16)
        product = lax.dot_general(kernel_weight, row_moments, NT, preferred_element_type=jnp.float32)
        top = 0
        for ref in out_refs:
            piece = product[top : top + ref.shape[0]]
            ref[...] = piece if start == 0 else ref[...] + piece
            top += ref.shape[0]


def expand_kernel(width, first_ref, second_ref, out_ref, held, full):
    share = out_ref.shape[0]
    total = first_ref[:share] + second_ref[...]
    where, _ = segments(width)
    tall = held.shape[0] // width
    for j in range(width):
        offset, first = where[j]
        held[j * tall : j * tall + share, first:width] = total[:, offset : offset + width - first]
    upper = lax.broadcasted_iota(jnp.int32, (width, width), 1) >= lax.broadcasted_iota(
        jnp.int32, (width, width), 0
    )
    for q in range(share):
        square = held[pl.ds(q, width, stride=tall), :][:, :width]
        whole = jnp.where(upper, square, square.T)
        full[pl.ds(q, width, stride=tall), :] = jnp.concatenate([whole] * (LANES // width), axis=1)
    for j in range(width):
        lane = j * width % LANES
        out_ref[:, j * width : (j + 1) * width] = full[j * tall : j * tall + share, lane : lane + width]


def per_device(row_leaves, covariates, query_leaves, leaf_sizes):
    axis = "rows"
    count = lax.axis_size(axis)
    trees, local_rows = row_leaves.shape
    width = covariates.shape[0]
    queries = query_leaves.shape[1]
    leaves = leaf_sizes.shape[1]
    share = queries // count
    _, columns = segments(width)
    least = local_rows * count // leaves // 2
    unit = float(trees * least * 512)
    order = block_order(count)
    groups = stages(count)

    half = queries // 2
    step = math.gcd(local_rows, 256)
    arguments = [
        pltpu.with_memory_space_constraint(a, pltpu.HBM)
        for a in (row_leaves, covariates, query_leaves, leaf_sizes)
    ]
    held, sent = pl.pallas_call(
        functools.partial(moments_kernel, axis, order, unit, step),
        out_shape=[pltpu.VMEM((half, columns), jnp.float32)] * 2,
        in_specs=[pl.BlockSpec(memory_space=pltpu.HBM)] * len(arguments),
        scratch_shapes=[pltpu.VMEM(a.shape, a.dtype) for a in arguments]
        + [pltpu.SemaphoreType.DMA((2,)), pltpu.SemaphoreType.DMA((local_rows // step, 2))],
        compiler_params=pltpu.CompilerParams(vmem_limit_bytes=40 << 20),
        cost_estimate=pl.CostEstimate(
            flops=2 * queries * columns * local_rows,
            bytes_accessed=1 << 20,
            transcendentals=0,
        ),
        name="moments",
    )(*arguments)

    def permute(array, shift):
        return lax.ppermute(array, axis, [(i, i ^ shift) for i in range(count)])

    first, second = held, permute(sent, groups[0][0])
    for group in groups[1:]:
        total = first[: second.shape[0]] + second
        blocks = 1 << len(group)
        size = total.shape[0] // blocks
        arrived = []
        for s in range(1, blocks):
            shift = sum(b for i, b in enumerate(group) if (s >> i) & 1)
            arrived.append(permute(total[s * size : (s + 1) * size], shift))
        first = total
        for extra in arrived[:-1]:
            first = first[:size] + extra
        second = arrived[-1]

    return pl.pallas_call(
        functools.partial(expand_kernel, width),
        out_shape=jax.ShapeDtypeStruct((share, width * width), jnp.float32),
        scratch_shapes=[pltpu.VMEM((width * 8, LANES), jnp.float32)] * 2,
        compiler_params=pltpu.CompilerParams(vmem_limit_bytes=4 << 20),
        name="expand",
    )(first, second)


def solution(mesh):
    return jax.shard_map(
        per_device,
        mesh=mesh,
        in_specs=(
            P(None, ("groups", "rows")),
            P(None, ("groups", "rows")),
            P(None, "groups"),
            P("groups", None),
        ),
        out_specs=P(("groups", "rows"), None),
        check_vma=False,
    )
```

```python
import functools
import math

import jax
import jax.numpy as jnp
from jax import lax
from jax.experimental import pallas as pl
from jax.experimental.pallas import tpu as pltpu
from jax.sharding import PartitionSpec as P

SUB = 8
LANES = 128
NT = (((1,), (1,)), ((), ()))


def segments(width):
    found, offset = [], 0
    for j in range(width):
        first = j // SUB * SUB
        found.append((offset, first))
        offset += width - first
    return found, offset


def stages(count):
    bits = [1 << i for i in range(count.bit_length() - 1)]
    rest = bits[1:]
    return [bits[:1]] * (count > 1) + [rest[i : i + 2] for i in range(0, len(rest), 2)]


def block_order(count):
    order = [0]
    for group in reversed(stages(count)):
        shifts = [sum(b for i, b in enumerate(group) if (s >> i) & 1) for s in range(1 << len(group))]
        order = [s | p for s in shifts for p in order]
    return order


def moments_kernel(axis, order, unit, step, rl_hbm, x_hbm, ql_hbm, ls_hbm, *refs):
    *out_refs, rl_ref, x_ref, ql_ref, ls_ref, turned_ref, small, large = refs
    trees, rows = rl_ref.shape
    width = x_ref.shape[0]
    queries = ql_ref.shape[1]
    share = queries // len(order)
    me = lax.axis_index(axis)

    copies = [
        pltpu.make_async_copy(ql_hbm, ql_ref, small.at[0]),
        pltpu.make_async_copy(ls_hbm, ls_ref, small.at[1]),
    ]
    copies += [
        pltpu.make_async_copy(rl_hbm, rl_ref, large.at[0]),
        pltpu.make_async_copy(x_hbm, x_ref, large.at[1]),
    ]
    for copy in copies:
        copy.start()
    for copy in copies[:2]:
        copy.wait()

    span = max(queries, LANES)
    place = lax.broadcasted_iota(jnp.int32, (trees, span), 1)
    block = jnp.zeros((trees, span), jnp.int32)
    for i in range(len(order).bit_length() - 1):
        block += ((place // share >> i) & 1) * order[1 << i]
    source = ((block ^ me) * share + place % share) % queries
    leaves = ql_ref[...]
    if queries < span:
        leaves = jnp.concatenate([leaves] * (span // queries), axis=1)
    inverse = 1.0 / (trees * ls_ref[...].astype(jnp.float32))
    leaf_parts, weight_parts = [], []
    for part in range(span // LANES):
        at = source[:, part * LANES : (part + 1) * LANES]
        taken = jnp.zeros((trees, LANES), jnp.int32)
        for piece in range(span // LANES):
            got = jnp.take_along_axis(leaves[:, piece * LANES : (piece + 1) * LANES], at % LANES, axis=1)
            taken = jnp.where(at // LANES == piece, got, taken)
        weight = jnp.take_along_axis(inverse, taken, axis=1).astype(jnp.bfloat16).astype(jnp.float32)
        leaf_parts.append(taken.T)
        weight_parts.append((weight.T * unit).astype(jnp.int32))
    leaf = jnp.concatenate(leaf_parts, 0)[:queries].astype(jnp.int16)
    weight = jnp.concatenate(weight_parts, 0)[:queries].astype(jnp.int16)

    for copy in copies[2:]:
        copy.wait()
    tall = 32
    turn = turned_ref.shape[1]
    for start in range(0, rows, step):
        here = slice(start, start + step)
        row_leaf = rl_ref[:, here].astype(jnp.int16)
        parts = []
        for top in range(0, queries, tall):
            total = jnp.zeros((tall, step), jnp.int16)
            for b in range(trees):
                want = jnp.broadcast_to(leaf[top : top + tall, b : b + 1], (tall, step))
                gives = jnp.broadcast_to(weight[top : top + tall, b : b + 1], (tall, step))
                have = jnp.broadcast_to(row_leaf[b : b + 1], (tall, step))
                total += jnp.where(have == want, gives, jnp.int16(0))
            parts.append((total.astype(jnp.float32) * (1.0 / unit)).astype(jnp.bfloat16))
        kernel_weight = jnp.concatenate(parts, 0)
        wide = x_ref[:, here].astype(jnp.float32)
        row_moments = jnp.concatenate([wide[j : j + 1] * wide[j // SUB * SUB :] for j in range(width)], 0)
        row_moments = row_moments.astype(jnp.bfloat16)
        turned_ref[...] = row_moments[:turn].T
        product = jnp.concatenate(
            [
                jnp.dot(kernel_weight, turned_ref[...], preferred_element_type=jnp.float32),
                lax.dot_general(kernel_weight, row_moments[turn:], NT, preferred_element_type=jnp.float32),
            ],
            1,
        )
        top = 0
        for ref in out_refs:
            piece = product[top : top + ref.shape[0]]
            ref[...] = piece if start == 0 else ref[...] + piece
            top += ref.shape[0]


def expand_kernel(width, first_ref, second_ref, out_ref, held, full):
    share = out_ref.shape[0]
    total = first_ref[:share] + second_ref[...]
    where, _ = segments(width)
    tall = held.shape[0] // width
    for j in range(width):
        offset, first = where[j]
        held[j * tall : j * tall + share, first:width] = total[:, offset : offset + width - first]
    upper = lax.broadcasted_iota(jnp.int32, (width, width), 1) >= lax.broadcasted_iota(
        jnp.int32, (width, width), 0
    )
    for q in range(share):
        square = held[pl.ds(q, width, stride=tall), :][:, :width]
        whole = jnp.where(upper, square, square.T)
        full[pl.ds(q, width, stride=tall), :] = jnp.concatenate([whole] * (LANES // width), axis=1)
    for j in range(width):
        lane = j * width % LANES
        out_ref[:, j * width : (j + 1) * width] = full[j * tall : j * tall + share, lane : lane + width]


def per_device(row_leaves, covariates, query_leaves, leaf_sizes):
    axis = "rows"
    count = lax.axis_size(axis)
    trees, local_rows = row_leaves.shape
    width = covariates.shape[0]
    queries = query_leaves.shape[1]
    leaves = leaf_sizes.shape[1]
    share = queries // count
    _, columns = segments(width)
    least = local_rows * count // leaves // 2
    unit = float(trees * least * 512)
    order = block_order(count)
    groups = stages(count)

    half = queries // 2
    step = math.gcd(local_rows, 256)
    turn = columns // 512 * 256 + 256
    arguments = [
        pltpu.with_memory_space_constraint(a, pltpu.HBM)
        for a in (row_leaves, covariates, query_leaves, leaf_sizes)
    ]
    held, sent = pl.pallas_call(
        functools.partial(moments_kernel, axis, order, unit, step),
        out_shape=[pltpu.VMEM((half, columns), jnp.float32)] * 2,
        in_specs=[pl.BlockSpec(memory_space=pltpu.HBM)] * len(arguments),
        scratch_shapes=[pltpu.VMEM(a.shape, a.dtype) for a in arguments]
        + [pltpu.VMEM((step, turn), jnp.bfloat16)]
        + [pltpu.SemaphoreType.DMA((2,))] * 2,
        compiler_params=pltpu.CompilerParams(vmem_limit_bytes=40 << 20),
        cost_estimate=pl.CostEstimate(
            flops=2 * queries * columns * local_rows,
            bytes_accessed=1 << 20,
            transcendentals=0,
        ),
        name="moments",
    )(*arguments)

    def permute(array, shift):
        return lax.ppermute(array, axis, [(i, i ^ shift) for i in range(count)])

    first, second = held, permute(sent, groups[0][0])
    for group in groups[1:]:
        total = first[: second.shape[0]] + second
        blocks = 1 << len(group)
        size = total.shape[0] // blocks
        arrived = []
        for s in range(1, blocks):
            shift = sum(b for i, b in enumerate(group) if (s >> i) & 1)
            arrived.append(permute(total[s * size : (s + 1) * size], shift))
        first = total
        for extra in arrived[:-1]:
            first = first[:size] + extra
        second = arrived[-1]

    return pl.pallas_call(
        functools.partial(expand_kernel, width),
        out_shape=jax.ShapeDtypeStruct((share, width * width), jnp.float32),
        scratch_shapes=[pltpu.VMEM((width * 8, LANES), jnp.float32)] * 2,
        compiler_params=pltpu.CompilerParams(vmem_limit_bytes=4 << 20),
        name="expand",
    )(first, second)


def solution(mesh):
    return jax.shard_map(
        per_device,
        mesh=mesh,
        in_specs=(
            P(None, ("groups", "rows")),
            P(None, ("groups", "rows")),
            P(None, "groups"),
            P("groups", None),
        ),
        out_specs=P(("groups", "rows"), None),
        check_vma=False,
    )
```

```python
import functools
import math
import operator

import jax
import jax.numpy as jnp
from jax import lax
from jax.experimental import pallas as pl
from jax.experimental.pallas import tpu as pltpu
from jax.sharding import PartitionSpec as P

SUB = 8
LANES = 128
NT = (((1,), (1,)), ((), ()))


def segments(width):
    found, offset = [], 0
    for j in range(width):
        first = j // SUB * SUB
        found.append((offset, first))
        offset += width - first
    return found, offset


def stages(count):
    bits = [1 << i for i in range(count.bit_length() - 1)]
    rest = bits[1:]
    found = [bits[:1]] * (count > 1)
    for i in range(0, len(rest), 2):
        pair = rest[i : i + 2]
        found.append([shift ^ 1 for shift in pair])
    return found


def combine(group, s):
    return functools.reduce(operator.xor, (shift for i, shift in enumerate(group) if (s >> i) & 1), 0)


def block_order(count):
    order = [0]
    for group in reversed(stages(count)):
        order = [combine(group, s) ^ p for s in range(1 << len(group)) for p in order]
    return order


def moments_kernel(axis, order, unit, step, rl_hbm, x_hbm, ql_hbm, ls_hbm, *refs):
    *out_refs, rl_ref, x_ref, ql_ref, ls_ref, turned_ref, small, large = refs
    trees, rows = rl_ref.shape
    width = x_ref.shape[0]
    queries = ql_ref.shape[1]
    share = queries // len(order)
    me = lax.axis_index(axis)

    copies = [
        pltpu.make_async_copy(ql_hbm, ql_ref, small.at[0]),
        pltpu.make_async_copy(ls_hbm, ls_ref, small.at[1]),
    ]
    copies += [
        pltpu.make_async_copy(rl_hbm, rl_ref, large.at[0]),
        pltpu.make_async_copy(x_hbm, x_ref, large.at[1]),
    ]
    for copy in copies:
        copy.start()
    for copy in copies[:2]:
        copy.wait()

    span = max(queries, LANES)
    place = lax.broadcasted_iota(jnp.int32, (trees, span), 1)
    block = jnp.zeros((trees, span), jnp.int32)
    for i in range(len(order).bit_length() - 1):
        block ^= ((place // share >> i) & 1) * order[1 << i]
    source = ((block ^ me) * share + place % share) % queries
    leaves = ql_ref[...]
    if queries < span:
        leaves = jnp.concatenate([leaves] * (span // queries), axis=1)
    inverse = 1.0 / (trees * ls_ref[...].astype(jnp.float32))
    leaf_parts, weight_parts = [], []
    for part in range(span // LANES):
        at = source[:, part * LANES : (part + 1) * LANES]
        taken = jnp.zeros((trees, LANES), jnp.int32)
        for piece in range(span // LANES):
            got = jnp.take_along_axis(leaves[:, piece * LANES : (piece + 1) * LANES], at % LANES, axis=1)
            taken = jnp.where(at // LANES == piece, got, taken)
        weight = jnp.take_along_axis(inverse, taken, axis=1).astype(jnp.bfloat16).astype(jnp.float32)
        leaf_parts.append(taken.T)
        weight_parts.append((weight.T * unit).astype(jnp.int32))
    leaf = jnp.concatenate(leaf_parts, 0)[:queries].astype(jnp.int16)
    weight = jnp.concatenate(weight_parts, 0)[:queries].astype(jnp.int16)

    for copy in copies[2:]:
        copy.wait()
    tall = 32
    turn = turned_ref.shape[1]
    for start in range(0, rows, step):
        here = slice(start, start + step)
        row_leaf = rl_ref[:, here].astype(jnp.int16)
        parts = []
        for top in range(0, queries, tall):
            total = jnp.zeros((tall, step), jnp.int16)
            for b in range(trees):
                want = jnp.broadcast_to(leaf[top : top + tall, b : b + 1], (tall, step))
                gives = jnp.broadcast_to(weight[top : top + tall, b : b + 1], (tall, step))
                have = jnp.broadcast_to(row_leaf[b : b + 1], (tall, step))
                total += jnp.where(have == want, gives, jnp.int16(0))
            parts.append((total.astype(jnp.float32) * (1.0 / unit)).astype(jnp.bfloat16))
        kernel_weight = jnp.concatenate(parts, 0)
        wide = x_ref[:, here].astype(jnp.float32)
        row_moments = jnp.concatenate([wide[j : j + 1] * wide[j // SUB * SUB :] for j in range(width)], 0)
        row_moments = row_moments.astype(jnp.bfloat16)
        turned_ref[...] = row_moments[:turn].T
        product = jnp.concatenate(
            [
                jnp.dot(kernel_weight, turned_ref[...], preferred_element_type=jnp.float32),
                lax.dot_general(kernel_weight, row_moments[turn:], NT, preferred_element_type=jnp.float32),
            ],
            1,
        )
        top = 0
        for ref in out_refs:
            piece = product[top : top + ref.shape[0]]
            ref[...] = piece if start == 0 else ref[...] + piece
            top += ref.shape[0]


def expand_kernel(width, first_ref, second_ref, out_ref, held, full):
    share = out_ref.shape[0]
    total = first_ref[:share] + second_ref[...]
    where, _ = segments(width)
    tall = held.shape[0] // width
    for j in range(width):
        offset, first = where[j]
        held[j * tall : j * tall + share, first:width] = total[:, offset : offset + width - first]
    upper = lax.broadcasted_iota(jnp.int32, (width, width), 1) >= lax.broadcasted_iota(
        jnp.int32, (width, width), 0
    )
    for q in range(share):
        square = held[pl.ds(q, width, stride=tall), :][:, :width]
        whole = jnp.where(upper, square, square.T)
        full[pl.ds(q, width, stride=tall), :] = jnp.concatenate([whole] * (LANES // width), axis=1)
    for j in range(width):
        lane = j * width % LANES
        out_ref[:, j * width : (j + 1) * width] = full[j * tall : j * tall + share, lane : lane + width]


def per_device(row_leaves, covariates, query_leaves, leaf_sizes):
    axis = "rows"
    count = lax.axis_size(axis)
    trees, local_rows = row_leaves.shape
    width = covariates.shape[0]
    queries = query_leaves.shape[1]
    leaves = leaf_sizes.shape[1]
    share = queries // count
    _, columns = segments(width)
    least = local_rows * count // leaves // 2
    unit = float(trees * least * 512)
    order = block_order(count)
    groups = stages(count)

    half = queries // 2
    step = math.gcd(local_rows, 256)
    turn = columns // 512 * 256 + 256
    arguments = [
        pltpu.with_memory_space_constraint(a, pltpu.HBM)
        for a in (row_leaves, covariates, query_leaves, leaf_sizes)
    ]
    held, sent = pl.pallas_call(
        functools.partial(moments_kernel, axis, order, unit, step),
        out_shape=[pltpu.VMEM((half, columns), jnp.float32)] * 2,
        in_specs=[pl.BlockSpec(memory_space=pltpu.HBM)] * len(arguments),
        scratch_shapes=[pltpu.VMEM(a.shape, a.dtype) for a in arguments]
        + [pltpu.VMEM((step, turn), jnp.bfloat16)]
        + [pltpu.SemaphoreType.DMA((2,))] * 2,
        compiler_params=pltpu.CompilerParams(vmem_limit_bytes=40 << 20),
        cost_estimate=pl.CostEstimate(
            flops=2 * queries * columns * local_rows,
            bytes_accessed=1 << 20,
            transcendentals=0,
        ),
        name="moments",
    )(*arguments)

    def permute(array, shift):
        return lax.ppermute(array, axis, [(i, i ^ shift) for i in range(count)])

    first, second = held, permute(sent, groups[0][0])
    for group in groups[1:]:
        total = first[: second.shape[0]] + second
        blocks = 1 << len(group)
        size = total.shape[0] // blocks
        arrived = []
        for s in range(1, blocks):
            arrived.append(permute(total[s * size : (s + 1) * size], combine(group, s)))
        first = total
        for extra in arrived[:-1]:
            first = first[:size] + extra
        second = arrived[-1]

    return pl.pallas_call(
        functools.partial(expand_kernel, width),
        out_shape=jax.ShapeDtypeStruct((share, width * width), jnp.float32),
        scratch_shapes=[pltpu.VMEM((width * 8, LANES), jnp.float32)] * 2,
        compiler_params=pltpu.CompilerParams(vmem_limit_bytes=4 << 20),
        name="expand",
    )(first, second)


def solution(mesh):
    return jax.shard_map(
        per_device,
        mesh=mesh,
        in_specs=(
            P(None, ("groups", "rows")),
            P(None, ("groups", "rows")),
            P(None, "groups"),
            P("groups", None),
        ),
        out_specs=P(("groups", "rows"), None),
        check_vma=False,
    )
```

```python
import functools
import math
import operator

import jax
import jax.numpy as jnp
from jax import lax
from jax.experimental import pallas as pl
from jax.experimental.pallas import tpu as pltpu
from jax.sharding import PartitionSpec as P

SUB = 8
LANES = 128
NT = (((1,), (1,)), ((), ()))


def segments(width):
    blocks = width // SUB
    found = []
    for j in range(width):
        block, row = divmod(j, SUB)
        first = block * SUB
        if 2 * block < blocks:
            found.append((j * width + first, first))
        elif 2 * block == blocks:
            window = first + row % (SUB // 2)
            found.append((window * width + (first if 2 * row < SUB else 0), first))
        else:
            found.append((((blocks - block) * SUB + row) * width, first))
    return found, (width + SUB) * width // 2


def stages(count):
    bits = [1 << i for i in range(count.bit_length() - 1)]
    rest = bits[1:]
    found = [bits[:1]] * (count > 1)
    for i in range(0, len(rest), 2):
        pair = rest[i : i + 2]
        found.append([shift ^ 1 for shift in pair])
    return found


def combine(group, s):
    return functools.reduce(operator.xor, (shift for i, shift in enumerate(group) if (s >> i) & 1), 0)


def block_order(count):
    order = [0]
    for group in reversed(stages(count)):
        order = [combine(group, s) ^ p for s in range(1 << len(group)) for p in order]
    return order


def moments_kernel(axis, order, unit, step, rl_hbm, x_hbm, ql_hbm, ls_hbm, *refs):
    *out_refs, rl_ref, x_ref, ql_ref, ls_ref, turned_ref, small, large = refs
    trees, rows = rl_ref.shape
    width = x_ref.shape[0]
    queries = ql_ref.shape[1]
    share = queries // len(order)
    me = lax.axis_index(axis)

    copies = [
        pltpu.make_async_copy(ql_hbm, ql_ref, small.at[0]),
        pltpu.make_async_copy(ls_hbm, ls_ref, small.at[1]),
    ]
    copies += [
        pltpu.make_async_copy(rl_hbm, rl_ref, large.at[0]),
        pltpu.make_async_copy(x_hbm, x_ref, large.at[1]),
    ]
    for copy in copies:
        copy.start()
    for copy in copies[:2]:
        copy.wait()

    span = max(queries, LANES)
    place = lax.broadcasted_iota(jnp.int32, (trees, span), 1)
    block = jnp.zeros((trees, span), jnp.int32)
    for i in range(len(order).bit_length() - 1):
        block ^= ((place // share >> i) & 1) * order[1 << i]
    source = ((block ^ me) * share + place % share) % queries
    leaves = ql_ref[...]
    if queries < span:
        leaves = jnp.concatenate([leaves] * (span // queries), axis=1)
    inverse = 1.0 / (trees * ls_ref[...].astype(jnp.float32))
    leaf_parts, weight_parts = [], []
    for part in range(span // LANES):
        at = source[:, part * LANES : (part + 1) * LANES]
        taken = jnp.zeros((trees, LANES), jnp.int32)
        for piece in range(span // LANES):
            got = jnp.take_along_axis(leaves[:, piece * LANES : (piece + 1) * LANES], at % LANES, axis=1)
            taken = jnp.where(at // LANES == piece, got, taken)
        weight = jnp.take_along_axis(inverse, taken, axis=1).astype(jnp.bfloat16).astype(jnp.float32)
        leaf_parts.append(taken.T)
        weight_parts.append((weight.T * unit).astype(jnp.int32))
    leaf = jnp.concatenate(leaf_parts, 0)[:queries].astype(jnp.int16)
    weight = jnp.concatenate(weight_parts, 0)[:queries].astype(jnp.int16)

    for copy in copies[2:]:
        copy.wait()
    tall = 16
    turn = turned_ref.shape[1]
    placed = sorted((offset, first, j) for j, (offset, first) in enumerate(segments(width)[0]))
    for start in range(0, rows, step):
        here = slice(start, start + step)
        row_leaf = rl_ref[:, here].astype(jnp.int16)
        parts = []
        for top in range(0, queries, tall):
            total = jnp.zeros((tall, step), jnp.int16)
            for b in range(trees):
                want = jnp.broadcast_to(leaf[top : top + tall, b : b + 1], (tall, step))
                gives = jnp.broadcast_to(weight[top : top + tall, b : b + 1], (tall, step))
                have = jnp.broadcast_to(row_leaf[b : b + 1], (tall, step))
                total += jnp.where(have == want, gives, jnp.int16(0))
            parts.append((total.astype(jnp.float32) * (1.0 / unit)).astype(jnp.bfloat16))
        kernel_weight = jnp.concatenate(parts, 0)
        wide = x_ref[:, here].astype(jnp.float32)
        row_moments = jnp.concatenate([wide[j : j + 1] * wide[first:] for _, first, j in placed], 0)
        row_moments = row_moments.astype(jnp.bfloat16)
        turned_ref[...] = row_moments[:turn].T
        product = jnp.concatenate(
            [
                jnp.dot(kernel_weight, turned_ref[...], preferred_element_type=jnp.float32),
                lax.dot_general(kernel_weight, row_moments[turn:], NT, preferred_element_type=jnp.float32),
            ],
            1,
        )
        top = 0
        for ref in out_refs:
            piece = product[top : top + ref.shape[0]]
            ref[...] = piece if start == 0 else ref[...] + piece
            top += ref.shape[0]


def expand_kernel(width, first_ref, second_ref, out_ref, held, full):
    share = out_ref.shape[0]
    total = first_ref[:share] + second_ref[...]
    where, _ = segments(width)
    tall = held.shape[0] // width
    for j in range(width):
        offset, first = where[j]
        held[j * tall : j * tall + share, first:width] = total[:, offset : offset + width - first]
    upper = lax.broadcasted_iota(jnp.int32, (width, width), 1) >= lax.broadcasted_iota(
        jnp.int32, (width, width), 0
    )
    for q in range(share):
        square = held[pl.ds(q, width, stride=tall), :][:, :width]
        whole = jnp.where(upper, square, square.T)
        full[pl.ds(q, width, stride=tall), :] = jnp.concatenate([whole] * (LANES // width), axis=1)
    copies = LANES // width
    for j in range(0, width, copies):
        rows = [full[(j + h) * tall : (j + h) * tall + share, h * width : (h + 1) * width] for h in range(copies)]
        out_ref[:, j * width : (j + copies) * width] = jnp.concatenate(rows, 1)


def per_device(row_leaves, covariates, query_leaves, leaf_sizes):
    axis = "rows"
    count = lax.axis_size(axis)
    trees, local_rows = row_leaves.shape
    width = covariates.shape[0]
    queries = query_leaves.shape[1]
    leaves = leaf_sizes.shape[1]
    share = queries // count
    _, columns = segments(width)
    least = local_rows * count // leaves // 2
    unit = float(trees * least * 512)
    order = block_order(count)
    groups = stages(count)

    half = queries // 2
    step = math.gcd(local_rows, 256)
    turn = columns // 512 * 256 + 256
    arguments = [
        pltpu.with_memory_space_constraint(a, pltpu.HBM)
        for a in (row_leaves, covariates, query_leaves, leaf_sizes)
    ]
    held, sent = pl.pallas_call(
        functools.partial(moments_kernel, axis, order, unit, step),
        out_shape=[pltpu.VMEM((half, columns), jnp.float32)] * 2,
        in_specs=[pl.BlockSpec(memory_space=pltpu.HBM)] * len(arguments),
        scratch_shapes=[pltpu.VMEM(a.shape, a.dtype) for a in arguments]
        + [pltpu.VMEM((step, turn), jnp.bfloat16)]
        + [pltpu.SemaphoreType.DMA((2,))] * 2,
        compiler_params=pltpu.CompilerParams(vmem_limit_bytes=40 << 20),
        cost_estimate=pl.CostEstimate(
            flops=2 * queries * columns * local_rows,
            bytes_accessed=1 << 20,
            transcendentals=0,
        ),
        name="moments",
    )(*arguments)

    def permute(array, shift):
        return lax.ppermute(array, axis, [(i, i ^ shift) for i in range(count)])

    first, second = held, permute(sent, groups[0][0])
    for group in groups[1:]:
        total = first[: second.shape[0]] + second
        blocks = 1 << len(group)
        size = total.shape[0] // blocks
        arrived = []
        for s in range(1, blocks):
            arrived.append(permute(total[s * size : (s + 1) * size], combine(group, s)))
        first = total
        for extra in arrived[:-1]:
            first = first[:size] + extra
        second = arrived[-1]

    return pl.pallas_call(
        functools.partial(expand_kernel, width),
        out_shape=jax.ShapeDtypeStruct((share, width * width), jnp.float32),
        scratch_shapes=[pltpu.VMEM((width * 8, LANES), jnp.float32)] * 2,
        compiler_params=pltpu.CompilerParams(vmem_limit_bytes=4 << 20),
        name="expand",
    )(first, second)


def solution(mesh):
    return jax.shard_map(
        per_device,
        mesh=mesh,
        in_specs=(
            P(None, ("groups", "rows")),
            P(None, ("groups", "rows")),
            P(None, "groups"),
            P("groups", None),
        ),
        out_specs=P(("groups", "rows"), None),
        check_vma=False,
    )
```

```python
import functools
import math
import operator

import jax
import jax.numpy as jnp
from jax import lax
from jax.experimental import pallas as pl
from jax.experimental.pallas import tpu as pltpu
from jax.sharding import PartitionSpec as P

SUB = 8
LANES = 128
NT = (((1,), (1,)), ((), ()))


def segments(width):
    blocks = width // SUB
    found = []
    for j in range(width):
        block, row = divmod(j, SUB)
        first = block * SUB
        if 2 * block < blocks:
            found.append((j * width + first, first))
        elif 2 * block == blocks:
            window = first + row % (SUB // 2)
            found.append((window * width + (first if 2 * row < SUB else 0), first))
        else:
            found.append((((blocks - block) * SUB + row) * width, first))
    return found, (width + SUB) * width // 2


def stages(count):
    bits = [1 << i for i in range(count.bit_length() - 1)]
    rest = bits[1:]
    found = [bits[:1]] * (count > 1)
    for i in range(0, len(rest), 2):
        pair = rest[i : i + 2]
        found.append([shift ^ 1 for shift in pair])
    return found


def combine(group, s):
    return functools.reduce(operator.xor, (shift for i, shift in enumerate(group) if (s >> i) & 1), 0)


def block_order(count):
    order = [0]
    for group in reversed(stages(count)):
        order = [combine(group, s) ^ p for s in range(1 << len(group)) for p in order]
    return order


def moments_kernel(axis, order, unit, step, rl_hbm, x_hbm, ql_hbm, ls_hbm, *refs):
    *out_refs, rl_ref, x_ref, ql_ref, ls_ref, t0, t1, s0, s1, small, large = refs
    turned_refs, straight_refs = (t0, t1), (s0, s1)
    trees, rows = rl_ref.shape
    width = x_ref.shape[0]
    queries = ql_ref.shape[1]
    share = queries // len(order)
    me = lax.axis_index(axis)

    copies = [
        pltpu.make_async_copy(ql_hbm, ql_ref, small.at[0]),
        pltpu.make_async_copy(ls_hbm, ls_ref, small.at[1]),
    ]
    copies += [
        pltpu.make_async_copy(rl_hbm, rl_ref, large.at[0]),
        pltpu.make_async_copy(x_hbm, x_ref, large.at[1]),
    ]
    for copy in copies:
        copy.start()
    for copy in copies[:2]:
        copy.wait()

    span = max(queries, LANES)
    place = lax.broadcasted_iota(jnp.int32, (trees, span), 1)
    block = jnp.zeros((trees, span), jnp.int32)
    for i in range(len(order).bit_length() - 1):
        block ^= ((place // share >> i) & 1) * order[1 << i]
    source = ((block ^ me) * share + place % share) % queries
    leaves = ql_ref[...]
    if queries < span:
        leaves = jnp.concatenate([leaves] * (span // queries), axis=1)
    inverse = 1.0 / (trees * ls_ref[...].astype(jnp.float32))
    leaf_parts, weight_parts = [], []
    for part in range(span // LANES):
        at = source[:, part * LANES : (part + 1) * LANES]
        taken = jnp.zeros((trees, LANES), jnp.int32)
        for piece in range(span // LANES):
            got = jnp.take_along_axis(leaves[:, piece * LANES : (piece + 1) * LANES], at % LANES, axis=1)
            taken = jnp.where(at // LANES == piece, got, taken)
        weight = jnp.take_along_axis(inverse, taken, axis=1).astype(jnp.bfloat16).astype(jnp.float32)
        leaf_parts.append(taken.T)
        weight_parts.append((weight.T * unit).astype(jnp.int32))
    leaf = jnp.concatenate(leaf_parts, 0)[:queries].astype(jnp.int16)
    weight = jnp.concatenate(weight_parts, 0)[:queries].astype(jnp.int16)

    for copy in copies[2:]:
        copy.wait()
    tall = 16
    turn = t0.shape[1]
    waiting = []

    def add(start, kernel_weight):
        slot = start // step % 2
        product = jnp.concatenate(
            [
                jnp.dot(kernel_weight, turned_refs[slot][...], preferred_element_type=jnp.float32),
                lax.dot_general(kernel_weight, straight_refs[slot][...], NT, preferred_element_type=jnp.float32),
            ],
            1,
        )
        top = 0
        for ref in out_refs:
            piece = product[top : top + ref.shape[0]]
            ref[...] = piece if start == 0 else ref[...] + piece
            top += ref.shape[0]

    placed = sorted((offset, first, j) for j, (offset, first) in enumerate(segments(width)[0]))
    for start in range(0, rows, step):
        here = slice(start, start + step)
        row_leaf = rl_ref[:, here].astype(jnp.int16)
        parts = []
        for top in range(0, queries, tall):
            total = jnp.zeros((tall, step), jnp.int16)
            for b in range(trees):
                want = jnp.broadcast_to(leaf[top : top + tall, b : b + 1], (tall, step))
                gives = jnp.broadcast_to(weight[top : top + tall, b : b + 1], (tall, step))
                have = jnp.broadcast_to(row_leaf[b : b + 1], (tall, step))
                total += jnp.where(have == want, gives, jnp.int16(0))
            parts.append((total.astype(jnp.float32) * (1.0 / unit)).astype(jnp.bfloat16))
        kernel_weight = jnp.concatenate(parts, 0)
        wide = x_ref[:, here].astype(jnp.float32)
        row_moments = jnp.concatenate([wide[j : j + 1] * wide[first:] for _, first, j in placed], 0)
        row_moments = row_moments.astype(jnp.bfloat16)
        turned_refs[start // step % 2][...] = row_moments[:turn].T
        straight_refs[start // step % 2][...] = row_moments[turn:]
        waiting.append((start, kernel_weight))
        if len(waiting) > 1:
            add(*waiting.pop(0))
    add(*waiting.pop(0))


def expand_kernel(width, first_ref, second_ref, out_ref, held, full):
    share = out_ref.shape[0]
    total = first_ref[:share] + second_ref[...]
    where, _ = segments(width)
    tall = held.shape[0] // width
    for j in range(width):
        offset, first = where[j]
        held[j * tall : j * tall + share, first:width] = total[:, offset : offset + width - first]
    upper = lax.broadcasted_iota(jnp.int32, (width, width), 1) >= lax.broadcasted_iota(
        jnp.int32, (width, width), 0
    )
    for q in range(share):
        square = held[pl.ds(q, width, stride=tall), :][:, :width]
        whole = jnp.where(upper, square, square.T)
        full[pl.ds(q, width, stride=tall), :] = jnp.concatenate([whole] * (LANES // width), axis=1)
    copies = LANES // width
    for j in range(0, width, copies):
        rows = [full[(j + h) * tall : (j + h) * tall + share, h * width : (h + 1) * width] for h in range(copies)]
        out_ref[:, j * width : (j + copies) * width] = jnp.concatenate(rows, 1)


def per_device(row_leaves, covariates, query_leaves, leaf_sizes):
    axis = "rows"
    count = lax.axis_size(axis)
    trees, local_rows = row_leaves.shape
    width = covariates.shape[0]
    queries = query_leaves.shape[1]
    leaves = leaf_sizes.shape[1]
    share = queries // count
    _, columns = segments(width)
    least = local_rows * count // leaves // 2
    unit = float(trees * least * 512)
    order = block_order(count)
    groups = stages(count)

    half = queries // 2
    step = math.gcd(local_rows, 256)
    turn = columns // 512 * 256 + 256
    arguments = [
        pltpu.with_memory_space_constraint(a, pltpu.HBM)
        for a in (row_leaves, covariates, query_leaves, leaf_sizes)
    ]
    held, sent = pl.pallas_call(
        functools.partial(moments_kernel, axis, order, unit, step),
        out_shape=[pltpu.VMEM((half, columns), jnp.float32)] * 2,
        in_specs=[pl.BlockSpec(memory_space=pltpu.HBM)] * len(arguments),
        scratch_shapes=[pltpu.VMEM(a.shape, a.dtype) for a in arguments]
        + [pltpu.VMEM((step, turn), jnp.bfloat16)] * 2
        + [pltpu.VMEM((columns - turn, step), jnp.bfloat16)] * 2
        + [pltpu.SemaphoreType.DMA((2,))] * 2,
        compiler_params=pltpu.CompilerParams(vmem_limit_bytes=40 << 20),
        cost_estimate=pl.CostEstimate(
            flops=2 * queries * columns * local_rows,
            bytes_accessed=1 << 20,
            transcendentals=0,
        ),
        name="moments",
    )(*arguments)

    def permute(array, shift):
        return lax.ppermute(array, axis, [(i, i ^ shift) for i in range(count)])

    first, second = held, permute(sent, groups[0][0])
    for group in groups[1:]:
        total = first[: second.shape[0]] + second
        blocks = 1 << len(group)
        size = total.shape[0] // blocks
        arrived = []
        for s in range(1, blocks):
            arrived.append(permute(total[s * size : (s + 1) * size], combine(group, s)))
        first = total
        for extra in arrived[:-1]:
            first = first[:size] + extra
        second = arrived[-1]

    return pl.pallas_call(
        functools.partial(expand_kernel, width),
        out_shape=jax.ShapeDtypeStruct((share, width * width), jnp.float32),
        scratch_shapes=[pltpu.VMEM((width * 8, LANES), jnp.float32)] * 2,
        compiler_params=pltpu.CompilerParams(vmem_limit_bytes=4 << 20),
        name="expand",
    )(first, second)


def solution(mesh):
    return jax.shard_map(
        per_device,
        mesh=mesh,
        in_specs=(
            P(None, ("groups", "rows")),
            P(None, ("groups", "rows")),
            P(None, "groups"),
            P("groups", None),
        ),
        out_specs=P(("groups", "rows"), None),
        check_vma=False,
    )
```
